256 devices in a mesh: grp: 4 (over x_lo, core), blk: 64 (over y, z, x_hi).
Axes of the slice: x: 4 (x_hi: 2, x_lo: 2; x = x_hi * 2 + x_lo), y: 4, z: 8, core: 2. Of those that a mesh axis runs over, the one named last changes fastest.
Arguments:
- image_emb: float32 [131072, 1152], P(('grp', 'blk')), may hold values from -0.2 to 0.2
- text_emb: float32 [131072, 1152], P(('grp', 'blk')), may hold values from -0.2 to 0.2
- logit_scale: float32 [1], replicated, may hold values from 8 to 32
- logit_bias: float32 [1], replicated, may hold values from -4 to -1
Outputs:
- image_grad: float32 [131072, 1152], P(('grp', 'blk'))
- text_grad: float32 [131072, 1152], P(('grp', 'blk'))
The draws below stay inside these ranges and needn't reach their ends.
All inputs are finite; a program needn't handle non-finite values.
Results may differ from the reference program's by a relative error of at most 0.006.
Values may be sent and summed in bfloat16 or wider, within the bound.
A program may use at most 64 MiB of HBM per device.

```python
import math
import jax
import jax.numpy as jnp
from jax import lax

D = 1152
TOK_DEV = 512
PAIRS = 131072
N_GRP = 4
N_BLK = 64


def levels(key, dims, cuts, smallest, largest):
    def one(position, blocks):
        heights = jax.random.uniform(jax.random.fold_in(jax.random.fold_in(key, 6), position), (blocks,), jnp.float32, smallest / len(cuts), largest / len(cuts))
        return jnp.repeat(jnp.exp(heights), dims[position] // blocks).reshape((-1,) + (1,) * (len(dims) - position - 1))

    loudness = one(*cuts[0])
    for cut in cuts[1:]:
        loudness = loudness * one(*cut)
    return loudness


def noise(rng, extent, width, limit, cuts=(), held_as=jnp.bfloat16):
    entries = jax.random.normal(rng, extent, jnp.float32) * width
    if len(cuts) > 0:
        entries = levels(rng, extent, cuts, -0.22, 0.18) * entries
    return jnp.clip(entries, min=-limit, max=limit).astype(held_as)


def setup_inputs(seed: int = 0) -> dict:
    splits = jax.random.split(jax.random.key(seed), 5)
    return {
        "image_emb": noise(splits[0], (PAIRS, D), 0.03, 0.2, ((0, 256),), jnp.float32),
        "text_emb": noise(splits[1], (PAIRS, D), 0.03, 0.2, ((0, 256),), jnp.float32),
        "logit_scale": jnp.clip(jnp.exp(jax.random.uniform(splits[2], (1,), jnp.float32, math.log(8.0), math.log(32.0))), 8.0, 32.0),
        "logit_bias": jnp.clip(jax.random.uniform(splits[3], (1,), jnp.float32, -4.0, -1.0), -4.0, -1.0),
    }


epsilon = 1e-06

def normalize(values):
    inverse = lax.rsqrt(lax.optimization_barrier(jnp.sum(values * values, axis=-1, keepdims=True)) + epsilon)
    return (values * inverse, inverse)

def project_back(unit, inverse, accum):
    return inverse * (accum - unit * lax.optimization_barrier(jnp.sum(unit * accum, axis=-1, keepdims=True)))

def tile_weights(images, texts, scale_value, bias_value, diagonal):
    logits = jnp.dot(images, texts.T, preferred_element_type=jnp.float32) * scale_value + bias_value
    if diagonal:
        labels = 2.0 * jnp.eye(images.shape[0], dtype=jnp.float32) - 1.0
    else:
        labels = -jnp.ones_like(logits)
    grads = -labels * jax.nn.sigmoid(-labels * logits)
    return (scale_value * grads).astype(jnp.bfloat16)

def reference(image_emb, text_emb, logit_scale, logit_bias):
    image_unit, image_inv = normalize(image_emb)
    text_unit, text_inv = normalize(text_emb)
    image_bf = image_unit.astype(jnp.bfloat16).reshape(N_GRP, N_BLK, TOK_DEV, D)
    text_bf = text_unit.astype(jnp.bfloat16).reshape(N_GRP, N_BLK, TOK_DEV, D)
    scale_value = logit_scale[0]
    bias_value = logit_bias[0]

    def one_block(block):
        group_idx = block // N_BLK
        slot_idx = block % N_BLK
        own_images = image_bf[group_idx, slot_idx]
        own_texts = text_bf[group_idx, slot_idx]
        weights = tile_weights(own_images, own_texts, scale_value, bias_value, True)
        image_acc = jnp.dot(weights, own_texts, preferred_element_type=jnp.float32)
        text_acc = jnp.dot(weights.T, own_images, preferred_element_type=jnp.float32)
        for offset in (1, 2, 3):
            visitor = text_bf[group_idx, (slot_idx - offset) % N_BLK]
            weights = tile_weights(own_images, visitor, scale_value, bias_value, False)
            image_acc = image_acc + jnp.dot(weights, visitor, preferred_element_type=jnp.float32)
            guest = image_bf[group_idx, (slot_idx + offset) % N_BLK]
            weights = tile_weights(guest, own_texts, scale_value, bias_value, False)
            text_acc = text_acc + jnp.dot(weights.T, guest, preferred_element_type=jnp.float32)
        visitor = text_bf[(group_idx - 1) % N_GRP, slot_idx]
        weights = tile_weights(own_images, visitor, scale_value, bias_value, False)
        image_acc = image_acc + jnp.dot(weights, visitor, preferred_element_type=jnp.float32)
        guest = image_bf[(group_idx + 1) % N_GRP, slot_idx]
        weights = tile_weights(guest, own_texts, scale_value, bias_value, False)
        text_acc = text_acc + jnp.dot(weights.T, guest, preferred_element_type=jnp.float32)
        return (image_acc, text_acc)
    image_acc, text_acc = lax.map(one_block, jnp.arange(N_GRP * N_BLK, dtype=jnp.int32))
    image_acc = image_acc.reshape(PAIRS, D)
    text_acc = text_acc.reshape(PAIRS, D)
    return (project_back(image_unit, image_inv, image_acc), project_back(text_unit, text_inv, text_acc))
```

```python
import functools

import jax
import jax.numpy as jnp
from jax import lax
from jax.experimental import pallas as pl
from jax.experimental.pallas import tpu as pltpu
from jax.sharding import PartitionSpec as P

EPSILON = 1e-6
MESH = pl.DeviceIdType.MESH
F32 = jnp.float32
BF16 = jnp.bfloat16
TEXT_PARTS = 8
IMAGE_PARTS = 4


def product(a, b, contract):
    return lax.dot_general(a, b, ((contract[:1], contract[1:]), ((), ())), preferred_element_type=F32)


def kernel(
    n_grp, n_blk, rows, scale_ref, bias_ref, image_hbm, text_hbm, image_out, text_out,
    image32, text32, image_inv, text_inv, texts, images, weights, text_acc, image_acc, group_acc,
    text_send, image_send, group_send, text_back, image_back, relay_back, group_back,
    load_sem, store_sem,
    direct_s, group_s, relay_s, image_s, text_back_s, image_back_s, group_back_s,
    visit_r, group_r, image_r, text_back_r, image_back_r, relay_back_r, group_back_r,
):
    g, c = lax.axis_index("grp"), lax.axis_index("blk")
    even = lax.rem(g, 2) == 0
    odd = jnp.logical_not(even)
    tr, ir = rows // TEXT_PARTS, rows // IMAGE_PARTS
    scale, bias = scale_ref[0], bias_ref[0]

    def at(dg, dc):
        return (lax.rem(g + (dg + n_grp), n_grp), lax.rem(c + (dc + n_blk), n_blk))

    def text_rows(k, base=0):
        return pl.ds(pl.multiple_of(base + k * tr, tr), tr)

    def image_rows(k, base=0):
        return pl.ds(pl.multiple_of(base + k * ir, ir), ir)

    def remote(src, dst, send, recv, k, device):
        return pltpu.make_async_remote_copy(
            src_ref=src, dst_ref=dst, send_sem=send.at[k], recv_sem=recv.at[k],
            device_id=device, device_id_type=MESH,
        )

    own, visit, guest = 0, rows, 2 * rows

    def direct_copy(k):
        return remote(texts.at[text_rows(k)], texts.at[text_rows(k, visit)], direct_s, visit_r, k, at(0, 1))

    def group_copy(k):
        return remote(texts.at[text_rows(k)], texts.at[text_rows(k, guest)], group_s, group_r, k, at(1, 0))

    def relay_copy(k):
        return remote(
            texts.at[text_rows(k, guest)], texts.at[text_rows(k, visit)], relay_s, visit_r, k, at(-1, 1)
        )

    def image_copy(k):
        return remote(images.at[image_rows(k)], images.at[image_rows(k, rows)], image_s, image_r, k, at(0, -2))

    def text_back_copy(k):
        return remote(text_send.at[text_rows(k)], text_back.at[text_rows(k)], text_back_s, text_back_r, k, at(0, -1))

    def via_back_copy(k):
        return remote(
            text_send.at[text_rows(k)], relay_back.at[text_rows(k)], text_back_s, relay_back_r, k, at(1, -1)
        )

    def sum_back_copy(k):
        return remote(group_send.at[text_rows(k)], text_back.at[text_rows(k)], group_back_s, text_back_r, k, at(-1, 0))

    def group_back_copy(k):
        return remote(
            group_send.at[text_rows(k)], group_back.at[text_rows(k)], group_back_s, group_back_r, k, at(-1, 0)
        )

    def image_back_copy(k):
        return remote(
            image_send.at[image_rows(k)], image_back.at[image_rows(k)], image_back_s, image_back_r, k, at(0, 2)
        )

    def text_load(k):
        return pltpu.make_async_copy(text_hbm.at[text_rows(k)], text32.at[text_rows(k)], load_sem.at[0, k])

    def image_load(k):
        return pltpu.make_async_copy(image_hbm.at[image_rows(k)], image32.at[image_rows(k)], load_sem.at[1, k])

    def text_store(k):
        return pltpu.make_async_copy(text32.at[text_rows(k)], text_out.at[text_rows(k)], store_sem.at[0, k])

    def image_store(k):
        return pltpu.make_async_copy(image32.at[image_rows(k)], image_out.at[image_rows(k)], store_sem.at[1, k])

    barrier = pltpu.get_barrier_semaphore()

    def greet(partners):
        for partner in partners:
            pl.semaphore_signal(barrier, inc=1, device_id=at(*partner), device_id_type=MESH)

    common = ((0, 2), (0, -2), (1, 0), (-1, 0))
    pl.when(even)(lambda: greet(common + ((0, 1), (0, -1), (-1, 1))))
    pl.when(odd)(lambda: greet(common + ((1, -1),)))

    for k in range(TEXT_PARTS):
        text_load(k).start()
        if k < IMAGE_PARTS:
            image_load(k).start()

    def normalize(raw, inv, out, where):
        values = raw[where, :]
        inverse = lax.rsqrt(jnp.sum(values * values, axis=-1, keepdims=True) + EPSILON)
        inv[where, :] = inverse
        out[where, :] = (values * inverse).astype(BF16)

    def text_ready(k):
        text_load(k).wait()
        normalize(text32, text_inv, texts, text_rows(k))

    def text_go(k):
        pl.when(even)(lambda: direct_copy(k).start())
        group_copy(k).start()

    text_ready(0)
    pl.semaphore_wait(barrier, jnp.where(even, 7, 5))
    text_go(0)

    def image_first(k, _):
        image_load(k).wait()
        normalize(image32, image_inv, images, image_rows(k))
        image_copy(k).start()

    def text_first(k, _):
        text_ready(k)
        text_go(k)

    image_first(0, None)
    lax.fori_loop(1, TEXT_PARTS, lambda k, _: text_first(k, _), None)
    lax.fori_loop(1, IMAGE_PARTS, lambda k, _: image_first(k, _), None)

    def weigh(logit, diagonal=None):
        logit = logit * scale + bias
        if diagonal is None:
            return (scale / (1.0 + jnp.exp(-logit))).astype(BF16)
        sign = jnp.where(diagonal, -1.0, 1.0).astype(F32)
        return ((sign * scale) / (1.0 + jnp.exp(-sign * logit))).astype(BF16)

    def group_step(k, _):
        mine, theirs = text_rows(k), text_rows(k, guest)
        logit = product(texts[mine, :], images[:rows, :], (1, 1))
        down = lax.broadcasted_iota(jnp.int32, logit.shape, 0) + k * tr
        across = lax.broadcasted_iota(jnp.int32, logit.shape, 1)
        weights[mine, :rows] = weigh(logit, down == across)

        group_copy(k).wait_recv()
        pl.when(even)(lambda: relay_copy(k).start())
        weight = weigh(product(texts[theirs, :], images[:rows, :], (1, 1)))
        weights[theirs, :rows] = weight
        part = product(weight, images[:rows, :], (1, 0))

        @pl.when(even)
        def _():
            group_acc[mine, :] = part

        @pl.when(odd)
        def _():
            group_send[mine, :] = part.astype(BF16)
            group_back_copy(k).start()

    lax.fori_loop(0, TEXT_PARTS, group_step, None)

    def visit_step(k, _):
        image_copy(k).wait_recv()
        there = image_rows(k, rows)
        weights[:rows, there] = weigh(product(texts[:rows, :], images[there, :], (1, 1)))
        for part in range(TEXT_PARTS // IMAGE_PARTS):
            direct_copy(k * (TEXT_PARTS // IMAGE_PARTS) + part).wait_recv()
        here = image_rows(k, visit)
        weights[here, :rows] = weigh(product(texts[here, :], images[:rows, :], (1, 1)))

    lax.fori_loop(0, IMAGE_PARTS, visit_step, None)

    def corner_step(k, _):
        here = image_rows(k, visit)
        weights[here, rows:] = weigh(product(texts[here, :], images[rows:, :], (1, 1)))

    lax.fori_loop(0, IMAGE_PARTS, corner_step, None)

    def back_step(k, _):
        for part in range(TEXT_PARTS // IMAGE_PARTS):
            j = k * (TEXT_PARTS // IMAGE_PARTS) + part
            text_send[text_rows(j), :] = product(weights[text_rows(j, visit), :], images[...], (1, 0)).astype(BF16)
            pl.when(even)(lambda: text_back_copy(j).start())
            pl.when(odd)(lambda: via_back_copy(j).start())
            if part == 0:
                there = image_rows(k, rows)
                image_send[image_rows(k), :] = product(
                    weights[: 2 * rows, there], texts[: 2 * rows, :], (0, 0)
                ).astype(BF16)
                image_back_copy(k).start()

    lax.fori_loop(0, IMAGE_PARTS, back_step, None)

    def rest_step(k, _):
        here = image_rows(k)
        text_acc[here, :] = product(weights[here, :], images[...], (1, 0))
        image_acc[here, :] = product(weights[:, here], texts[...], (0, 0))

    lax.fori_loop(0, IMAGE_PARTS, rest_step, None)

    def project(raw, inv, accum, where):
        inverse = inv[where, :]
        unit = raw[where, :] * inverse
        raw[where, :] = inverse * (accum - unit * jnp.sum(unit * accum, axis=-1, keepdims=True))

    def last_step(k, _):
        for part in range(TEXT_PARTS // IMAGE_PARTS):
            j = k * (TEXT_PARTS // IMAGE_PARTS) + part
            here = text_rows(j)

            @pl.when(even)
            def _():
                via_back_copy(j).wait_recv()
                group_send[here, :] = (group_acc[here, :] + relay_back[here, :].astype(F32)).astype(BF16)
                sum_back_copy(j).start()
                group_back_copy(j).wait_recv()
                text_acc[here, :] += group_back[here, :].astype(F32)

            text_back_copy(j).wait_recv()
            project(text32, text_inv, text_acc[here, :] + text_back[here, :].astype(F32), here)
            text_store(j).start()
        here = image_rows(k)
        image_back_copy(k).wait_recv()
        project(image32, image_inv, image_acc[here, :] + image_back[here, :].astype(F32), here)
        image_store(k).start()

    lax.fori_loop(0, IMAGE_PARTS, last_step, None)

    def text_done(k, _):
        group_copy(k).wait_send()
        text_back_copy(k).wait_send()
        group_back_copy(k).wait_send()

        @pl.when(even)
        def _():
            direct_copy(k).wait_send()
            relay_copy(k).wait_send()

        text_store(k).wait()

    lax.fori_loop(0, TEXT_PARTS, text_done, None)

    def image_done(k, _):
        image_copy(k).wait_send()
        image_back_copy(k).wait_send()
        image_store(k).wait()

    lax.fori_loop(0, IMAGE_PARTS, image_done, None)


def local(n_grp, n_blk, image_emb, text_emb, logit_scale, logit_bias):
    rows, width = image_emb.shape
    whole, bf = pltpu.VMEM((rows, width), F32), pltpu.VMEM((rows, width), BF16)
    text_sem, image_sem = pltpu.SemaphoreType.DMA((TEXT_PARTS,)), pltpu.SemaphoreType.DMA((IMAGE_PARTS,))
    out = jax.ShapeDtypeStruct((rows, width), F32)
    tile = 2 * rows * rows * width
    return pl.pallas_call(
        functools.partial(kernel, n_grp, n_blk, rows),
        out_shape=(out, out),
        in_specs=[pl.BlockSpec(memory_space=pltpu.SMEM)] * 2 + [pl.BlockSpec(memory_space=pl.ANY)] * 2,
        out_specs=(pl.BlockSpec(memory_space=pl.ANY),) * 2,
        scratch_shapes=[
            whole, whole, pltpu.VMEM((rows, 1), F32), pltpu.VMEM((rows, 1), F32),
            pltpu.VMEM((3 * rows, width), BF16), pltpu.VMEM((2 * rows, width), BF16),
            pltpu.VMEM((3 * rows, 2 * rows), BF16), whole, whole, whole,
            bf, bf, bf, bf, bf, bf, bf,
            pltpu.SemaphoreType.DMA((2, TEXT_PARTS)), pltpu.SemaphoreType.DMA((2, TEXT_PARTS)),
            text_sem, text_sem, text_sem, image_sem, text_sem, image_sem, text_sem,
            text_sem, text_sem, image_sem, text_sem, image_sem, text_sem, text_sem,
        ],
        cost_estimate=pl.CostEstimate(
            flops=15 * tile, bytes_accessed=16 * rows * width, transcendentals=5 * rows * rows
        ),
        compiler_params=pltpu.CompilerParams(
            collective_id=0, has_side_effects=True, vmem_limit_bytes=48 * 2**20
        ),
        name="contrast",
    )(logit_scale, logit_bias, image_emb, text_emb)


def solution(mesh):
    blocks = P(("grp", "blk"), None)
    return jax.shard_map(
        functools.partial(local, mesh.shape["grp"], mesh.shape["blk"]),
        mesh=mesh,
        in_specs=(blocks, blocks, P(), P()),
        out_specs=(blocks, blocks),
        check_vma=False,
    )
```

```python
import functools

import jax
import jax.numpy as jnp
from jax import lax
from jax.experimental import pallas as pl
from jax.experimental.pallas import tpu as pltpu
from jax.sharding import PartitionSpec as P

EPSILON = 1e-6
MESH = pl.DeviceIdType.MESH
F32 = jnp.float32
BF16 = jnp.bfloat16
TEXT_PARTS = 8
IMAGE_PARTS = 4
AHEAD = 2
IMAGE_HOLD = 3


def product(a, b, contract):
    return lax.dot_general(a, b, ((contract[:1], contract[1:]), ((), ())), preferred_element_type=F32)


def kernel(
    n_grp, n_blk, rows, scale_ref, bias_ref, image_hbm, text_hbm, image_out, text_out,
    image32, text32, image_inv, text_inv, texts, images, weights, text_acc, image_acc, group_acc,
    text_send, image_send, group_send, text_back, image_back, relay_back, group_back,
    load_sem, store_sem,
    direct_s, group_s, relay_s, image_s, text_back_s, image_back_s, group_back_s,
    visit_r, group_r, image_r, text_back_r, image_back_r, relay_back_r, group_back_r, ack_sem, go_sem,
):
    g, c = lax.axis_index("grp"), lax.axis_index("blk")
    even = lax.rem(g, 2) == 0
    odd = jnp.logical_not(even)
    even_place = lax.rem(c, 2) == 0
    odd_place = jnp.logical_not(even_place)
    tr, ir = rows // TEXT_PARTS, rows // IMAGE_PARTS
    scale, bias = scale_ref[0], bias_ref[0]

    def at(dg, dc):
        return (lax.rem(g + (dg + n_grp), n_grp), lax.rem(c + (dc + n_blk), n_blk))

    def text_rows(k, base=0):
        return pl.ds(pl.multiple_of(base + k * tr, tr), tr)

    def image_rows(k, base=0):
        return pl.ds(pl.multiple_of(base + k * ir, ir), ir)

    def remote(src, dst, send, recv, k, device):
        return pltpu.make_async_remote_copy(
            src_ref=src, dst_ref=dst, send_sem=send.at[k], recv_sem=recv.at[k],
            device_id=device, device_id_type=MESH,
        )

    own, visit, guest = 0, rows, 2 * rows

    def direct_copy(k):
        return remote(texts.at[text_rows(k)], texts.at[text_rows(k, visit)], direct_s, visit_r, k, at(0, 1))

    def group_copy(k):
        return remote(texts.at[text_rows(k)], texts.at[text_rows(k, guest)], group_s, group_r, k, at(1, 0))

    def relay_copy(k):
        return remote(
            texts.at[text_rows(k, guest)], texts.at[text_rows(k, visit)], relay_s, visit_r, k, at(-1, 1)
        )

    def image_copy(k):
        return remote(images.at[image_rows(k)], images.at[image_rows(k, rows)], image_s, image_r, k, at(0, -2))

    def text_back_copy(k):
        return remote(text_send.at[text_rows(k)], text_back.at[text_rows(k)], text_back_s, text_back_r, k, at(0, -1))

    def via_back_copy(k):
        return remote(
            text_send.at[text_rows(k)], relay_back.at[text_rows(k)], text_back_s, relay_back_r, k, at(1, -1)
        )

    def sum_back_copy(k):
        return remote(group_send.at[text_rows(k)], text_back.at[text_rows(k)], group_back_s, text_back_r, k, at(-1, 0))

    def group_back_copy(k):
        return remote(
            group_send.at[text_rows(k)], group_back.at[text_rows(k)], group_back_s, group_back_r, k, at(-1, 0)
        )

    def image_back_copy(k):
        return remote(
            image_send.at[image_rows(k)], image_back.at[image_rows(k)], image_back_s, image_back_r, k, at(0, 2)
        )

    def text_load(k):
        return pltpu.make_async_copy(text_hbm.at[text_rows(k)], text32.at[text_rows(k)], load_sem.at[0, k])

    def image_load(k):
        return pltpu.make_async_copy(image_hbm.at[image_rows(k)], image32.at[image_rows(k)], load_sem.at[1, k])

    def text_store(k):
        return pltpu.make_async_copy(text32.at[text_rows(k)], text_out.at[text_rows(k)], store_sem.at[0, k])

    def image_store(k):
        return pltpu.make_async_copy(image32.at[image_rows(k)], image_out.at[image_rows(k)], store_sem.at[1, k])

    barrier = pltpu.get_barrier_semaphore()

    def signal(semaphore, partners):
        for partner in partners:
            pl.semaphore_signal(semaphore, inc=1, device_id=at(*partner), device_id_type=MESH)

    pl.when(even)(lambda: signal(barrier, ((1, 0), (-1, 0), (0, -1), (0, -2))))
    pl.when(odd)(lambda: signal(barrier, ((1, 0), (-1, 0), (0, -2), (1, -1), (-1, -2))))

    for k in range(IMAGE_PARTS):
        for j in range(TEXT_PARTS // IMAGE_PARTS):
            text_load(k * (TEXT_PARTS // IMAGE_PARTS) + j).start()
        image_load(k).start()

    def normalize(raw, inv, out, where):
        values = raw[where, :]
        inverse = lax.rsqrt(jnp.sum(values * values, axis=-1, keepdims=True) + EPSILON)
        inv[where, :] = inverse
        out[where, :] = (values * inverse).astype(BF16)

    def text_ready(k):
        text_load(k).wait()
        normalize(text32, text_inv, texts, text_rows(k))

    def text_go(k):
        group_copy(k).start()

    text_ready(0)
    pl.semaphore_wait(barrier, jnp.where(even, 6, 3))
    text_go(0)
    pl.when(even)(lambda: signal(ack_sem, ((0, 1), (0, 2), (-1, 1))))
    pl.when(odd)(lambda: signal(ack_sem, ((0, 2),)))

    def each(parts, step):
        lax.fori_loop(0, parts, lambda k, _: step(k), None)

    def image_ready(k):
        image_load(k).wait()
        normalize(image32, image_inv, images, image_rows(k))

    def text_first(k):
        text_ready(k)
        text_go(k)

    several = TEXT_PARTS // IMAGE_PARTS

    def both_first(k, _):
        each(several, lambda j: text_first(k * several + j))
        image_ready(k)
        pl.when(odd)(lambda: image_copy(k).start())

    image_ready(0)
    pl.semaphore_wait(ack_sem, 2)
    pl.when(odd)(lambda: image_copy(0).start())
    lax.fori_loop(1, several, lambda k, _: text_first(k), None)
    lax.fori_loop(1, IMAGE_PARTS, both_first, None)


    def weigh(logit, diagonal=None):
        logit = logit * scale + bias
        if diagonal is None:
            return (scale / (1.0 + jnp.exp(-logit))).astype(BF16)
        sign = jnp.where(diagonal, -1.0, 1.0).astype(F32)
        return ((sign * scale) / (1.0 + jnp.exp(-sign * logit))).astype(BF16)

    def score(text_at, text_n, image_at, image_n):
        t, i = pl.ds(text_at, text_n), pl.ds(image_at, image_n)
        weights[t, i] = weigh(product(texts[t, :], images[i, :], (1, 1)))

    logit = product(texts[:rows, :], images[:rows, :], (1, 1))
    down = lax.broadcasted_iota(jnp.int32, logit.shape, 0)
    across = lax.broadcasted_iota(jnp.int32, logit.shape, 1)
    weights[:rows, :rows] = weigh(logit, down == across)

    half = rows // 2

    def guest_half(h):
        score(guest + h * half, half, 0, rows)
        return product(weights[pl.ds(guest + h * half, half), :rows], images[:rows, :], (1, 0))

    def images_arrive(h):
        for k in range(h * IMAGE_PARTS // 2, (h + 1) * IMAGE_PARTS // 2):
            image_copy(k).wait_recv()

    def texts_arrive(h):
        for k in range(h * TEXT_PARTS // 2, (h + 1) * TEXT_PARTS // 2):
            direct_copy(k).wait_recv()

    def text_return(h):
        block = pl.ds(visit + h * half, half)
        text_send[pl.ds(h * half, half), :] = product(weights[block, :], images[...], (1, 0)).astype(BF16)

    def image_return(h):
        block = pl.ds(rows + h * half, half)
        image_send[pl.ds(h * half, half), :] = product(
            weights[: 2 * rows, block], texts[: 2 * rows, :], (0, 0)
        ).astype(BF16)

    def relay_step(k, _):
        group_copy(k).wait_recv()
        relay_copy(k).start()

        @pl.when(k == IMAGE_HOLD)
        def _():
            each(IMAGE_PARTS, lambda k: image_copy(k).start())

    def relay_back_step(k, _):
        mine = text_rows(k)
        via_back_copy(k).wait_recv()
        group_send[mine, :] = (group_acc[mine, :] + relay_back[mine, :].astype(F32)).astype(BF16)
        sum_back_copy(k).start()
        pl.when(k + AHEAD < TEXT_PARTS)(lambda: text_back_copy(k + AHEAD).start())

    def project(raw, inv, accum, where):
        inverse = inv[where, :]
        unit = raw[where, :] * inverse
        raw[where, :] = inverse * (accum - unit * jnp.sum(unit * accum, axis=-1, keepdims=True))

    def text_last(k):
        here = text_rows(k)

        @pl.when(even)
        def _():
            group_back_copy(k).wait_recv()
            text_acc[here, :] += group_back[here, :].astype(F32)

        text_back_copy(k).wait_recv()
        project(text32, text_inv, text_acc[here, :] + text_back[here, :].astype(F32), here)
        text_store(k).start()

    def image_last(k, _):
        here = image_rows(k)
        image_back_copy(k).wait_recv()
        project(image32, image_inv, image_acc[here, :] + image_back[here, :].astype(F32), here)
        image_store(k).start()

    def image_sum(k):
        here = image_rows(k)
        image_acc[here, :] = product(weights[:, here], texts[...], (0, 0))

    @pl.when(odd)
    def _():
        each(TEXT_PARTS, lambda k: group_copy(k).wait_recv())
        for h in range(2):
            group_send[pl.ds(h * half, half), :] = guest_half(h).astype(BF16)
        each(TEXT_PARTS, lambda k: group_back_copy(k).start())
        images_arrive(0)
        images_arrive(1)
        score(own, rows, rows, rows)
        texts_arrive(0)
        score(visit, half, 0, 2 * rows)
        text_return(0)
        texts_arrive(1)
        score(visit + half, half, 0, 2 * rows)
        text_return(1)
        pl.when(odd_place)(lambda: each(TEXT_PARTS, lambda k: via_back_copy(k).start()))
        image_return(0)
        image_return(1)
        pl.when(even_place)(lambda: each(IMAGE_PARTS, lambda k: image_back_copy(k).start()))
        text_acc[...] = product(weights[:rows, :], images[...], (1, 0))
        pl.semaphore_wait(go_sem, 1)
        pl.when(even_place)(lambda: each(TEXT_PARTS, lambda k: via_back_copy(k).start()))
        pl.when(odd_place)(lambda: each(IMAGE_PARTS, lambda k: image_back_copy(k).start()))

        lax.fori_loop(0, IMAGE_PARTS, lambda k, _: image_sum(k), None)
        lax.fori_loop(0, TEXT_PARTS - 1, lambda k, _: text_last(k), None)
        lax.fori_loop(0, IMAGE_PARTS, image_last, None)
        text_last(TEXT_PARTS - 1)

    @pl.when(even)
    def _():
        for h in range(2):
            lax.fori_loop(h * TEXT_PARTS // 2, (h + 1) * TEXT_PARTS // 2, relay_step, None)
            if h == 1:
                each(TEXT_PARTS - 1, lambda k: relay_copy(k).wait_send())
                each(TEXT_PARTS, lambda k: direct_copy(k).start())
            group_acc[pl.ds(h * half, half), :] = guest_half(h)
        images_arrive(0)
        score(own, rows, rows, half)
        texts_arrive(0)
        score(visit, half, 0, rows + half)
        relay_copy(TEXT_PARTS - 1).wait_send()
        each(TEXT_PARTS, lambda k: direct_copy(k).wait_send())
        pl.when(even_place)(lambda: signal(go_sem, ((0, 2), (1, 2))))
        pl.when(odd_place)(lambda: signal(go_sem, ((1, 0),)))
        images_arrive(1)
        score(visit, half, rows + half, half)
        text_return(0)
        pl.when(even_place)(lambda: pl.semaphore_wait(go_sem, 1))
        each(AHEAD, lambda k: text_back_copy(k).start())
        score(own, rows, rows + half, half)
        texts_arrive(1)
        score(visit + half, half, 0, 2 * rows)
        text_return(1)
        relay_back_step(0, None)
        relay_back_step(1, None)
        image_return(0)
        each(IMAGE_PARTS // 2, lambda k: image_back_copy(k).start())
        relay_back_step(2, None)
        image_return(1)
        each(IMAGE_PARTS // 2, lambda k: image_back_copy(k + IMAGE_PARTS // 2).start())
        relay_back_step(3, None)
        text_acc[...] = product(weights[:rows, :], images[...], (1, 0))

        def even_step(k, _):
            relay_back_step(k + TEXT_PARTS - IMAGE_PARTS, None)
            image_sum(k)
            text_last(k)

        lax.fori_loop(0, IMAGE_PARTS, even_step, None)
        lax.fori_loop(IMAGE_PARTS, TEXT_PARTS - 1, lambda k, _: text_last(k), None)
        lax.fori_loop(0, IMAGE_PARTS, image_last, None)
        text_last(TEXT_PARTS - 1)

    def text_done(k, _):
        group_copy(k).wait_send()
        text_back_copy(k).wait_send()
        group_back_copy(k).wait_send()


        text_store(k).wait()

    lax.fori_loop(0, TEXT_PARTS, text_done, None)

    def image_done(k, _):
        image_copy(k).wait_send()
        image_back_copy(k).wait_send()
        image_store(k).wait()

    lax.fori_loop(0, IMAGE_PARTS, image_done, None)


def local(n_grp, n_blk, image_emb, text_emb, logit_scale, logit_bias):
    rows, width = image_emb.shape
    whole, bf = pltpu.VMEM((rows, width), F32), pltpu.VMEM((rows, width), BF16)
    text_sem, image_sem = pltpu.SemaphoreType.DMA((TEXT_PARTS,)), pltpu.SemaphoreType.DMA((IMAGE_PARTS,))
    out = jax.ShapeDtypeStruct((rows, width), F32)
    tile = 2 * rows * rows * width
    return pl.pallas_call(
        functools.partial(kernel, n_grp, n_blk, rows),
        out_shape=(out, out),
        in_specs=[pl.BlockSpec(memory_space=pltpu.SMEM)] * 2 + [pl.BlockSpec(memory_space=pl.ANY)] * 2,
        out_specs=(pl.BlockSpec(memory_space=pl.ANY),) * 2,
        scratch_shapes=[
            whole, whole, pltpu.VMEM((rows, 1), F32), pltpu.VMEM((rows, 1), F32),
            pltpu.VMEM((3 * rows, width), BF16), pltpu.VMEM((2 * rows, width), BF16),
            pltpu.VMEM((3 * rows, 2 * rows), BF16), whole, whole, whole,
            bf, bf, bf, bf, bf, bf, bf,
            pltpu.SemaphoreType.DMA((2, TEXT_PARTS)), pltpu.SemaphoreType.DMA((2, TEXT_PARTS)),
            text_sem, text_sem, text_sem, image_sem, text_sem, image_sem, text_sem,
            text_sem, text_sem, image_sem, text_sem, image_sem, text_sem, text_sem, pltpu.SemaphoreType.REGULAR, pltpu.SemaphoreType.REGULAR,
        ],
        cost_estimate=pl.CostEstimate(
            flops=15 * tile, bytes_accessed=16 * rows * width, transcendentals=5 * rows * rows
        ),
        compiler_params=pltpu.CompilerParams(
            collective_id=0, has_side_effects=True, vmem_limit_bytes=48 * 2**20
        ),
        name="contrast",
    )(logit_scale, logit_bias, image_emb, text_emb)


def solution(mesh):
    blocks = P(("grp", "blk"), None)
    return jax.shard_map(
        functools.partial(local, mesh.shape["grp"], mesh.shape["blk"]),
        mesh=mesh,
        in_specs=(blocks, blocks, P(), P()),
        out_specs=(blocks, blocks),
        check_vma=False,
    )
```

```python
import functools

import jax
import jax.numpy as jnp
from jax import lax
from jax.experimental import pallas as pl
from jax.experimental.pallas import tpu as pltpu
from jax.sharding import PartitionSpec as P

EPSILON = 1e-6
MESH = pl.DeviceIdType.MESH
F32 = jnp.float32
BF16 = jnp.bfloat16
TEXT_PARTS = 8
IMAGE_PARTS = 4
AHEAD = 2
IMAGE_HOLD = 3


def product(a, b, contract):
    return lax.dot_general(a, b, ((contract[:1], contract[1:]), ((), ())), preferred_element_type=F32)


def kernel(
    n_grp, n_blk, rows, scale_ref, bias_ref, image_hbm, text_hbm, image_out, text_out,
    image32, text32, image_inv, text_inv, texts, images, weights, text_acc, image_acc, group_acc,
    text_send, image_send, group_send, text_back, image_back, relay_back, group_back,
    load_sem, store_sem,
    direct_s, group_s, relay_s, image_s, text_back_s, image_back_s, group_back_s,
    visit_r, group_r, image_r, text_back_r, image_back_r, relay_back_r, group_back_r, ack_sem, go_sem,
):
    g, c = lax.axis_index("grp"), lax.axis_index("blk")
    even = lax.rem(g, 2) == 0
    odd = jnp.logical_not(even)
    even_place = lax.rem(c, 2) == 0
    odd_place = jnp.logical_not(even_place)
    tr, ir = rows // TEXT_PARTS, rows // IMAGE_PARTS
    scale, bias = scale_ref[0], bias_ref[0]

    def at(dg, dc):
        return (lax.rem(g + (dg + n_grp), n_grp), lax.rem(c + (dc + n_blk), n_blk))

    def text_rows(k, base=0):
        return pl.ds(pl.multiple_of(base + k * tr, tr), tr)

    def image_rows(k, base=0):
        return pl.ds(pl.multiple_of(base + k * ir, ir), ir)

    def remote(src, dst, send, recv, k, device):
        return pltpu.make_async_remote_copy(
            src_ref=src, dst_ref=dst, send_sem=send.at[k], recv_sem=recv.at[k],
            device_id=device, device_id_type=MESH,
        )

    own, visit, guest = 0, rows, 2 * rows

    def direct_copy(k):
        return remote(texts.at[text_rows(k)], texts.at[text_rows(k, visit)], direct_s, visit_r, k, at(0, 1))

    def group_copy(k):
        return remote(texts.at[text_rows(k)], texts.at[text_rows(k, guest)], group_s, group_r, k, at(1, 0))

    def relay_copy(k):
        return remote(
            texts.at[text_rows(k, guest)], texts.at[text_rows(k, visit)], relay_s, visit_r, k, at(-1, 1)
        )

    def image_copy(k):
        return remote(images.at[image_rows(k)], images.at[image_rows(k, rows)], image_s, image_r, k, at(0, -2))

    def text_back_copy(k):
        return remote(text_send.at[text_rows(k)], text_back.at[text_rows(k)], text_back_s, text_back_r, k, at(0, -1))

    def via_back_copy(k):
        return remote(
            text_send.at[text_rows(k)], relay_back.at[text_rows(k)], text_back_s, relay_back_r, k, at(1, -1)
        )

    def sum_back_copy(k):
        return remote(group_send.at[text_rows(k)], text_back.at[text_rows(k)], group_back_s, text_back_r, k, at(-1, 0))

    def group_back_copy(k):
        return remote(
            group_send.at[text_rows(k)], group_back.at[text_rows(k)], group_back_s, group_back_r, k, at(-1, 0)
        )

    def image_back_copy(k):
        return remote(
            image_send.at[image_rows(k)], image_back.at[image_rows(k)], image_back_s, image_back_r, k, at(0, 2)
        )

    def text_load(k):
        return pltpu.make_async_copy(text_hbm.at[text_rows(k)], text32.at[text_rows(k)], load_sem.at[0, k])

    def image_load(k):
        return pltpu.make_async_copy(image_hbm.at[image_rows(k)], image32.at[image_rows(k)], load_sem.at[1, k])

    def text_store(k):
        return pltpu.make_async_copy(text32.at[text_rows(k)], text_out.at[text_rows(k)], store_sem.at[0, k])

    def image_store(k):
        return pltpu.make_async_copy(image32.at[image_rows(k)], image_out.at[image_rows(k)], store_sem.at[1, k])

    barrier = pltpu.get_barrier_semaphore()

    def signal(semaphore, partners):
        for partner in partners:
            pl.semaphore_signal(semaphore, inc=1, device_id=at(*partner), device_id_type=MESH)

    pl.when(even)(lambda: signal(barrier, ((1, 0), (-1, 0), (0, -1), (0, -2))))
    pl.when(odd)(lambda: signal(barrier, ((1, 0), (-1, 0), (0, -2), (1, -1), (-1, -2))))

    for k in range(IMAGE_PARTS):
        for j in range(TEXT_PARTS // IMAGE_PARTS):
            text_load(k * (TEXT_PARTS // IMAGE_PARTS) + j).start()
        image_load(k).start()

    def normalize(raw, inv, out, where):
        values = raw[where, :]
        inverse = lax.rsqrt(jnp.sum(values * values, axis=-1, keepdims=True) + EPSILON)
        inv[where, :] = inverse
        out[where, :] = (values * inverse).astype(BF16)

    def text_ready(k):
        text_load(k).wait()
        normalize(text32, text_inv, texts, text_rows(k))

    def text_go(k):
        group_copy(k).start()

    text_ready(0)
    pl.semaphore_wait(barrier, jnp.where(even, 6, 3))
    text_go(0)
    pl.when(even)(lambda: signal(ack_sem, ((0, 1), (0, 2), (-1, 1))))
    pl.when(odd)(lambda: signal(ack_sem, ((0, 2),)))

    def each(parts, step):
        lax.fori_loop(0, parts, lambda k, _: step(k), None)

    def image_ready(k):
        image_load(k).wait()
        normalize(image32, image_inv, images, image_rows(k))

    def text_first(k):
        text_ready(k)
        text_go(k)

    several = TEXT_PARTS // IMAGE_PARTS

    def both_first(k, _):
        each(several, lambda j: text_first(k * several + j))
        image_ready(k)
        pl.when(odd)(lambda: image_copy(k).start())

    image_ready(0)
    pl.semaphore_wait(ack_sem, 2)
    pl.when(odd)(lambda: image_copy(0).start())
    lax.fori_loop(1, several, lambda k, _: text_first(k), None)
    lax.fori_loop(1, IMAGE_PARTS, both_first, None)


    def weigh(logit, diagonal=None):
        logit = logit * scale + bias
        if diagonal is None:
            return (scale / (1.0 + jnp.exp(-logit))).astype(BF16)
        sign = jnp.where(diagonal, -1.0, 1.0).astype(F32)
        return ((sign * scale) / (1.0 + jnp.exp(-sign * logit))).astype(BF16)

    def score(text_at, text_n, image_at, image_n):
        t, i = pl.ds(text_at, text_n), pl.ds(image_at, image_n)
        weights[t, i] = weigh(product(texts[t, :], images[i, :], (1, 1)))

    logit = product(texts[:rows, :], images[:rows, :], (1, 1))
    down = lax.broadcasted_iota(jnp.int32, logit.shape, 0)
    across = lax.broadcasted_iota(jnp.int32, logit.shape, 1)
    weights[:rows, :rows] = weigh(logit, down == across)

    half = rows // 2

    def guest_half(h):
        score(guest + h * half, half, 0, rows)
        return product(weights[pl.ds(guest + h * half, half), :rows], images[:rows, :], (1, 0))

    def images_arrive(h):
        for k in range(h * IMAGE_PARTS // 2, (h + 1) * IMAGE_PARTS // 2):
            image_copy(k).wait_recv()

    def texts_arrive(h):
        for k in range(h * TEXT_PARTS // 2, (h + 1) * TEXT_PARTS // 2):
            direct_copy(k).wait_recv()

    def text_return(h):
        block = pl.ds(visit + h * half, half)
        text_send[pl.ds(h * half, half), :] = product(weights[block, :], images[...], (1, 0)).astype(BF16)

    def image_return(h):
        block = pl.ds(rows + h * half, half)
        image_send[pl.ds(h * half, half), :] = product(
            weights[: 2 * rows, block], texts[: 2 * rows, :], (0, 0)
        ).astype(BF16)

    def relay_step(k, _):
        group_copy(k).wait_recv()
        relay_copy(k).start()

        @pl.when(k == IMAGE_HOLD)
        def _():
            each(IMAGE_PARTS, lambda k: image_copy(k).start())

    def relay_back_step(k, _):
        mine = text_rows(k)
        via_back_copy(k).wait_recv()
        group_send[mine, :] = (group_acc[mine, :] + relay_back[mine, :].astype(F32)).astype(BF16)
        sum_back_copy(k).start()
        pl.when(k + AHEAD < TEXT_PARTS)(lambda: text_back_copy(k + AHEAD).start())

    def project(raw, inv, accum, where):
        inverse = inv[where, :]
        unit = raw[where, :] * inverse
        raw[where, :] = inverse * (accum - unit * jnp.sum(unit * accum, axis=-1, keepdims=True))

    def text_last(k):
        here = text_rows(k)

        @pl.when(even)
        def _():
            group_back_copy(k).wait_recv()
            text_acc[here, :] += group_back[here, :].astype(F32)

        text_back_copy(k).wait_recv()
        project(text32, text_inv, text_acc[here, :] + text_back[here, :].astype(F32), here)
        text_store(k).start()

    def image_last(k, _):
        here = image_rows(k)
        image_back_copy(k).wait_recv()
        project(image32, image_inv, image_acc[here, :] + image_back[here, :].astype(F32), here)
        image_store(k).start()

    def image_sum(k):
        here = image_rows(k)
        image_acc[here, :] = product(weights[:, here], texts[...], (0, 0))

    @pl.when(odd)
    def _():
        each(TEXT_PARTS, lambda k: group_copy(k).wait_recv())
        for h in range(2):
            group_send[pl.ds(h * half, half), :] = guest_half(h).astype(BF16)
        each(TEXT_PARTS, lambda k: group_back_copy(k).start())
        images_arrive(0)
        images_arrive(1)
        score(own, rows, rows, rows)
        texts_arrive(0)
        score(visit, half, 0, 2 * rows)
        text_return(0)
        texts_arrive(1)
        score(visit + half, half, 0, 2 * rows)
        text_return(1)
        pl.when(odd_place)(lambda: each(TEXT_PARTS, lambda k: via_back_copy(k).start()))
        image_return(0)
        image_return(1)
        pl.when(even_place)(lambda: each(IMAGE_PARTS, lambda k: image_back_copy(k).start()))
        text_acc[...] = product(weights[:rows, :], images[...], (1, 0))
        pl.semaphore_wait(go_sem, 1)
        pl.when(even_place)(lambda: each(TEXT_PARTS, lambda k: via_back_copy(k).start()))
        pl.when(odd_place)(lambda: each(IMAGE_PARTS, lambda k: image_back_copy(k).start()))

        lax.fori_loop(0, IMAGE_PARTS, lambda k, _: image_sum(k), None)
        lax.fori_loop(0, TEXT_PARTS - 1, lambda k, _: text_last(k), None)
        lax.fori_loop(0, IMAGE_PARTS, image_last, None)
        text_last(TEXT_PARTS - 1)

    @pl.when(even)
    def _():
        for h in range(2):
            lax.fori_loop(h * TEXT_PARTS // 2, (h + 1) * TEXT_PARTS // 2, relay_step, None)
            if h == 1:
                each(TEXT_PARTS - 1, lambda k: relay_copy(k).wait_send())
                each(TEXT_PARTS, lambda k: direct_copy(k).start())
            group_acc[pl.ds(h * half, half), :] = guest_half(h)
        images_arrive(0)
        score(own, rows, rows, half)
        texts_arrive(0)
        score(visit, half, 0, rows + half)
        relay_copy(TEXT_PARTS - 1).wait_send()
        each(TEXT_PARTS, lambda k: direct_copy(k).wait_send())
        pl.when(even_place)(lambda: signal(go_sem, ((0, 2), (1, 2))))
        pl.when(odd_place)(lambda: signal(go_sem, ((1, 0),)))
        images_arrive(1)
        score(visit, half, rows + half, half)
        text_return(0)
        pl.when(even_place)(lambda: pl.semaphore_wait(go_sem, 1))
        each(AHEAD, lambda k: text_back_copy(k).start())
        score(own, rows, rows + half, half)
        texts_arrive(1)
        score(visit + half, half, 0, 2 * rows)
        text_return(1)
        relay_back_step(0, None)
        relay_back_step(1, None)
        image_return(0)
        each(IMAGE_PARTS // 2, lambda k: image_back_copy(k).start())
        relay_back_step(2, None)
        image_return(1)
        each(IMAGE_PARTS // 2, lambda k: image_back_copy(k + IMAGE_PARTS // 2).start())
        relay_back_step(3, None)
        text_acc[...] = product(weights[:rows, :], images[...], (1, 0))

        def even_step(k, _):
            relay_back_step(k + TEXT_PARTS - IMAGE_PARTS, None)
            image_sum(k)
            text_last(k)

        lax.fori_loop(0, IMAGE_PARTS, even_step, None)
        lax.fori_loop(IMAGE_PARTS, TEXT_PARTS - 1, lambda k, _: text_last(k), None)
        lax.fori_loop(0, IMAGE_PARTS, image_last, None)
        text_last(TEXT_PARTS - 1)

    def text_done(k, _):
        group_copy(k).wait_send()
        text_back_copy(k).wait_send()
        group_back_copy(k).wait_send()


        text_store(k).wait()

    lax.fori_loop(0, TEXT_PARTS, text_done, None)

    def image_done(k, _):
        image_copy(k).wait_send()
        image_back_copy(k).wait_send()
        image_store(k).wait()

    lax.fori_loop(0, IMAGE_PARTS, image_done, None)


def hand_over(rows, image_in, text_in, image_out, text_out, sem):
    part = rows // IMAGE_PARTS
    copies = [
        pltpu.make_async_copy(src.at[pl.ds(k * part, part)], dst.at[pl.ds(k * part, part)], sem.at[i, k])
        for i, (src, dst) in enumerate(((image_in, image_out), (text_in, text_out)))
        for k in range(IMAGE_PARTS)
    ]
    for copy in copies:
        copy.start()
    for copy in copies:
        copy.wait()


def local(n_grp, n_blk, image_emb, text_emb, logit_scale, logit_bias):
    rows, width = image_emb.shape
    whole, bf = pltpu.VMEM((rows, width), F32), pltpu.VMEM((rows, width), BF16)
    text_sem, image_sem = pltpu.SemaphoreType.DMA((TEXT_PARTS,)), pltpu.SemaphoreType.DMA((IMAGE_PARTS,))
    out = jax.ShapeDtypeStruct((rows, width), F32)
    tile = 2 * rows * rows * width
    grads = pl.pallas_call(
        functools.partial(kernel, n_grp, n_blk, rows),
        out_shape=(out, out),
        in_specs=[pl.BlockSpec(memory_space=pltpu.SMEM)] * 2 + [pl.BlockSpec(memory_space=pl.ANY)] * 2,
        out_specs=(pl.BlockSpec(memory_space=pl.ANY),) * 2,
        scratch_shapes=[
            whole, whole, pltpu.VMEM((rows, 1), F32), pltpu.VMEM((rows, 1), F32),
            pltpu.VMEM((3 * rows, width), BF16), pltpu.VMEM((2 * rows, width), BF16),
            pltpu.VMEM((3 * rows, 2 * rows), BF16), whole, whole, whole,
            bf, bf, bf, bf, bf, bf, bf,
            pltpu.SemaphoreType.DMA((2, TEXT_PARTS)), pltpu.SemaphoreType.DMA((2, TEXT_PARTS)),
            text_sem, text_sem, text_sem, image_sem, text_sem, image_sem, text_sem,
            text_sem, text_sem, image_sem, text_sem, image_sem, text_sem, text_sem, pltpu.SemaphoreType.REGULAR, pltpu.SemaphoreType.REGULAR,
        ],
        cost_estimate=pl.CostEstimate(
            flops=15 * tile, bytes_accessed=16 * rows * width, transcendentals=5 * rows * rows
        ),
        compiler_params=pltpu.CompilerParams(
            collective_id=0, has_side_effects=True, vmem_limit_bytes=48 * 2**20
        ),
        name="contrast",
    )(logit_scale, logit_bias, image_emb, text_emb)


    return pl.pallas_call(
        functools.partial(hand_over, rows),
        out_shape=(out, out),
        in_specs=[pl.BlockSpec(memory_space=pl.ANY)] * 2,
        out_specs=(pl.BlockSpec(memory_space=pl.ANY),) * 2,
        scratch_shapes=[pltpu.SemaphoreType.DMA((2, IMAGE_PARTS))],
        cost_estimate=pl.CostEstimate(flops=0, bytes_accessed=8 * rows * width, transcendentals=0),
        compiler_params=pltpu.CompilerParams(vmem_limit_bytes=2**20),
        name="hand_over",
    )(*grads)


def solution(mesh):
    blocks = P(("grp", "blk"), None)
    return jax.shard_map(
        functools.partial(local, mesh.shape["grp"], mesh.shape["blk"]),
        mesh=mesh,
        in_specs=(blocks, blocks, P(), P()),
        out_specs=(blocks, blocks),
        check_vma=False,
    )
```
